256 devices in a mesh: pair: 32 (over z, x), aux: 8 (over y, core).
Axes of the slice: x: 4, y: 4, z: 8, core: 2. Of those that a mesh axis runs over, the one named last changes fastest.
Arguments:
- amplitudes: bfloat16 [128, 128, 128], P('pair'), may hold values from -0.59765625 to 0.59765625
- coefficients: bfloat16 [128, 512, 128], P('pair'), may hold values from -0.375 to 0.375
- energies: float32 [128, 128], P('pair'), may hold values from 0.2 to 3
- pair_shift: float32 [128], P('pair'), may hold values from -3 to -1
- pno_count: int32 [128], P('pair'), may hold values from 64 to 128
- coupled_pairs: int32 [128, 16], P('pair'), may hold values from 0 to 127, as said below
- coupling_weight: float32 [128, 16], P('pair'), may hold values from -1.5 to 1.5
- slab_one: bfloat16 [128, 24576, 128], P('pair', 'aux'), may hold values from -0.47851562 to 0.47851562
- slab_two: bfloat16 [128, 24576, 128], P('pair', 'aux'), may hold values from -0.47851562 to 0.47851562
Outputs:
- residual: float32 [128, 128, 128], P('pair')
The draws below stay inside these ranges and needn't reach their ends.
Inputs may be any that keep to these rules, and one draw needn't show every extreme that they name: `coupled_pairs`: pair q is owned by index q // 4 of the pair axis. Among the 64 couplings of one owner's pairs, at most 3 name pairs of any one owner, and in every draw exactly 3 of each owner's couplings name pairs of some one owner (two of them may name the same pair).
All inputs are finite; a program needn't handle non-finite values.
Results may differ from the reference program's by a relative error of at most 0.003.
Values may be sent and summed in bfloat16 or wider, within the bound.
No kernel may reach another device: no remote copies, remote signals or barrier semaphores. Data moves between devices by JAX's collectives and lax.ppermute only.
A program may use at most 128 MiB of HBM per device.

```python
import jax
import jax.numpy as jnp
from jax import lax

V = 128
NV = 512
NAUX = 24576
P_DEV = 4
K = 16
PAIRS = 128
CAP = 3


def draw_coupled_pairs(key, part):
    key = jax.random.fold_in(key, 11)
    owner_total = PAIRS // P_DEV
    slot_total = owner_total * CAP
    needed = P_DEV * K

    def one_owner(owner_index, owner_key):
        key_order, key_local, key_mix = jax.random.split(owner_key, 3)
        shuffled = jax.random.permutation(key_order, slot_total)
        ranking = jnp.argsort(shuffled)
        forced = (owner_index + 1) % owner_total
        order_key = jnp.where(jnp.arange(slot_total) // CAP == forced, -1, ranking)
        chosen = jnp.argsort(order_key, stable=True)[:needed]
        target = chosen // CAP
        local_slot = jax.random.randint(key_local, (needed,), 0, P_DEV)
        linked = target * P_DEV + local_slot
        linked = linked[jax.random.permutation(key_mix, needed)]
        return linked.reshape(P_DEV, K)
    owner_keys = jax.random.split(key, owner_total)
    result = jax.vmap(one_owner)(jnp.arange(owner_total), owner_keys)
    return result.reshape(PAIRS, K).astype(jnp.int32)


def set_ends(values, key, low, top_value):
    dims = values.shape
    index_at = [jax.random.randint(jax.random.fold_in(key, axis), (), 0, dims[axis]) for axis in range(len(dims))]
    values = values.at[tuple(index_at)].set(low)
    longest = dims.index(max(dims))
    index_at[longest] = (index_at[longest] + 1) % dims[longest]
    return values.at[tuple(index_at)].set(top_value)


def level_of(own_key, shape, shards, low, high):
    loudness = 1.0
    for dim, shards_of in shards:
        heights = jax.random.uniform(jax.random.fold_in(jax.random.fold_in(own_key, 6), dim), (shards_of,), jnp.float32, low / len(shards), high / len(shards))
        loudness = loudness * jnp.repeat(jnp.exp(heights), shape[dim] // shards_of).reshape((-1,) + (1,) * (len(shape) - 1 - dim))
    return loudness


def normal_values(stream_key, shape, deviation, bound, pieces=(), held_as=jnp.bfloat16):
    array = deviation * jax.random.normal(stream_key, shape, jnp.float32)
    if pieces:
        array = array * level_of(stream_key, shape, pieces, -0.22, 0.18)
    return jnp.clip(array, -bound, bound).astype(held_as)


def setup_inputs(seed: int = 0) -> dict:
    key_of = jax.random.split(jax.random.key(seed), 10)
    return {
        "amplitudes": normal_values(key_of[0], (PAIRS, V, V), 0.1, 0.59765625, ((0, 32),)),
        "coefficients": normal_values(key_of[1], (PAIRS, NV, V), ((NV * V) ** -0.25), 0.375, ((0, 32),)),
        "energies": jnp.clip(0.2 + 2.8 * jax.random.uniform(key_of[2], (PAIRS, V), jnp.float32) ** level_of(key_of[2], (PAIRS, V), ((0, 32),), -0.2, 0.2), 0.2, 3.0),
        "pair_shift": jnp.clip(-3.0 + 2.0 * jax.random.uniform(key_of[3], (PAIRS,), jnp.float32) ** level_of(key_of[3], (PAIRS,), ((0, 32),), -0.2, 0.2), -3.0, -1.0),
        "pno_count": set_ends(jax.random.randint(key_of[4], (PAIRS,), V // 2, V + 1), jax.random.fold_in(key_of[4], 1), V // 2, V).astype(jnp.int32),
        "coupled_pairs": draw_coupled_pairs(jax.random.fold_in(key_of[9], 71), 0),
        "coupling_weight": normal_values(key_of[6], (PAIRS, K), 0.3, 1.5, ((0, 32),), jnp.float32),
        "slab_one": normal_values(key_of[7], (PAIRS, NAUX, V), (NAUX ** -0.25), 0.47851562, ((0, 32), (1, 8))),
        "slab_two": normal_values(key_of[8], (PAIRS, NAUX, V), (NAUX ** -0.25), 0.47851562, ((0, 32), (1, 8))),
    }


def project(own_coef, far_coef, far_amplitude):
    intersection = jnp.einsum("nv,knw->kvw", own_coef.astype(jnp.float32), far_coef.astype(jnp.float32)).astype(jnp.bfloat16)
    half_way = jnp.einsum("kac,kcd->kad", intersection.astype(jnp.float32), far_amplitude.astype(jnp.float32)).astype(jnp.bfloat16)
    return jnp.einsum("kad,kbd->kab", half_way.astype(jnp.float32), intersection.astype(jnp.float32)).astype(jnp.bfloat16)


def reference(amplitudes, coefficients, energies, pair_shift, pno_count, coupled_pairs, coupling_weight, slab_one, slab_two):
    pno_width = amplitudes.shape[1]

    def one_pair(items):
        own_amplitude, own_coef, energy, shift_value, used_count, linked, link_weight, first_slab, second_slab = items
        far_amplitude = amplitudes[linked]
        far_coef = coefficients[linked]
        projected = project(own_coef, far_coef, far_amplitude)
        coupling = jnp.sum(link_weight[:, None, None] * projected.astype(jnp.float32), axis=0)
        exchange = jnp.dot(first_slab.T, second_slab, preferred_element_type=jnp.float32)
        amp_float = own_amplitude.astype(jnp.float32)
        kernel_prod = jnp.dot(exchange, amp_float, precision=lax.Precision.HIGHEST)
        quadratic = jnp.dot(amp_float.T, kernel_prod, precision=lax.Precision.HIGHEST)
        diagonal = (energy[:, None] + energy[None, :] - shift_value) * amp_float
        summed = exchange + diagonal + quadratic - coupling
        inside = jnp.arange(pno_width) < used_count
        return jnp.where(inside[:, None] & inside[None, :], summed, jnp.float32(0.0)).astype(jnp.float32)

    return lax.map(one_pair, (amplitudes, coefficients, energies, pair_shift, pno_count, coupled_pairs, coupling_weight, slab_one, slab_two))
```

```python
import jax
import jax.numpy as jnp
from jax import lax
from jax.experimental import pallas as pl
from jax.experimental.pallas import tpu as pltpu
from jax.sharding import Mesh
from jax.sharding import PartitionSpec as P

NX, NY, NC = 4, 4, 2
ROWS = 16


def ring(size, step):
    return [(i, (i + step) % size) for i in range(size)]


def prepare_kernel(where, coef, amp, meta, z_out, x_out):
    y, c = where[2], where[3]
    nz = z_out.shape[0]
    half = coef.shape[1] // NC
    amp_half = amp.shape[1] // NC
    v = amp.shape[2]
    coef_part = coef[y, pl.ds(pl.multiple_of(c * half, half), half), :]
    amp_part = amp[y, pl.ds(pl.multiple_of(c * amp_half, amp_half), amp_half), :]
    for d in range(nz):
        z_out[d, :half, :] = coef_part
        z_out[d, half:, :] = amp_part
    for s in range(2):
        x_out[s * v : (s + 1) * v, :] = coef[2 * c + s].T
    x_out[2 * v : 2 * v + ROWS, :] = jnp.zeros((ROWS, x_out.shape[1]), x_out.dtype)
    x_out[2 * v : 2 * v + ROWS, :v] = meta[...]


def couple_kernel(
    where, p0, p1, p2, p3, q_mine, q_other, own, away, meta_f, meta_i, sm_f, sm_i, pick, acc, amp_q, sem
):
    x, y, c = where[1], where[2], where[3]
    v = q_mine.shape[2]
    half = p0.shape[1] // NC
    amp_half = v // NC
    parts = (p0, p1, p2, p3)
    for r, ref in enumerate(parts):
        rows = ref[2 * v : 2 * v + ROWS, :v].astype(jnp.float32)[:8]
        meta_f[r] = rows
        meta_i[r] = rows.astype(jnp.int32)
    copy_f = pltpu.make_async_copy(meta_f, sm_f, sem.at[0])
    copy_i = pltpu.make_async_copy(meta_i, sm_i, sem.at[1])
    copy_f.start()
    copy_i.start()
    acc[...] = jnp.zeros_like(acc)
    copy_f.wait()
    copy_i.wait()
    for r in range(NX):
        for s in range(2):

            def scan(k, found):
                pair_id = sm_i[r, c, s * 64 + k]
                owner = pair_id // 4
                hit = (pair_id % 4 == y) & (owner % NX == x)
                pick[0, found] = k
                pick[1, found] = owner // NX
                return found + hit.astype(jnp.int32)

            found = lax.fori_loop(0, 16, scan, 0)

            def one(j, carry):
                k = pick[0, j]
                zq = pick[1, j]
                base = s * 64 + 16 + k
                weight = sm_f[r, c, base] + sm_f[r, c, base + 16] + sm_f[r, c, base + 32]
                left = parts[r]
                mine_at = pl.multiple_of(c * half, half)
                other_at = pl.multiple_of((1 - c) * half, half)
                inter = jnp.dot(
                    left[s * v : (s + 1) * v, pl.ds(mine_at, half)],
                    q_mine[zq, :half, :],
                    preferred_element_type=jnp.float32,
                )
                inter += jnp.dot(
                    left[s * v : (s + 1) * v, pl.ds(other_at, half)],
                    q_other[zq, :half, :],
                    preferred_element_type=jnp.float32,
                )
                inter = inter.astype(jnp.bfloat16)
                amp_q[pl.ds(pl.multiple_of(c * amp_half, amp_half), amp_half), :] = q_mine[zq, half:, :]
                amp_q[pl.ds(pl.multiple_of((1 - c) * amp_half, amp_half), amp_half), :] = q_other[
                    zq, half:, :
                ]
                mid = jnp.dot(inter, amp_q[...], preferred_element_type=jnp.float32)
                mid = mid.astype(jnp.bfloat16)
                proj = lax.dot_general(
                    mid, inter, (((1,), (1,)), ((), ())), preferred_element_type=jnp.float32
                )
                acc[r, s] += weight * proj.astype(jnp.bfloat16).astype(jnp.float32)
                return carry

            lax.fori_loop(0, found, one, 0)
    own[...] = acc[0]
    for r in range(1, NX):
        away[r - 1] = acc[r].astype(jnp.bfloat16)


def split_weight(weight):
    first = lax.reduce_precision(weight, 8, 7)
    second = lax.reduce_precision(weight - first, 8, 7)
    third = lax.reduce_precision(weight - first - second, 8, 7)
    return first, second, third


def shards(
    amplitudes,
    coefficients,
    energies,
    pair_shift,
    pno_count,
    coupled_pairs,
    coupling_weight,
    slab_one,
    slab_two,
):
    pairs, v, _ = amplitudes.shape
    nv = coefficients.shape[1]
    nz = lax.axis_size("z")
    where = jnp.stack([lax.axis_index(a) for a in ("z", "x", "y", "c")]).astype(jnp.int32)
    c = where[3]
    smem = pl.BlockSpec(memory_space=pltpu.SMEM)
    vmem = pl.BlockSpec(memory_space=pltpu.VMEM)

    meta = jnp.concatenate(
        [coupled_pairs.astype(jnp.float32), *split_weight(coupling_weight)], axis=1
    ).astype(jnp.bfloat16)
    meta = jnp.pad(meta.reshape(2, 2 * meta.shape[1]), ((0, ROWS - 2), (0, 0)))
    z_block, x_block = pl.pallas_call(
        prepare_kernel,
        out_shape=(
            jax.ShapeDtypeStruct((nz, (nv + v) // NC, v), jnp.bfloat16),
            jax.ShapeDtypeStruct((2 * v + ROWS, nv), jnp.bfloat16),
        ),
        in_specs=[smem, vmem, vmem, vmem],
        out_specs=(vmem, vmem),
        name="prepare",
    )(where, coefficients, amplitudes, meta)
    x_parts = [x_block] + [lax.ppermute(x_block, "x", ring(NX, k)) for k in (1, 2, 3)]
    q_mine = lax.all_to_all(z_block, "z", split_axis=0, concat_axis=0, tiled=True)
    q_other = lax.ppermute(q_mine, "c", ring(NC, 1))

    exchange = jnp.einsum("pqa,pqb->pab", slab_one, slab_two, preferred_element_type=jnp.float32)
    gone = lax.dynamic_slice_in_dim(exchange, 2 * (1 - c), 2, 0)
    kept = lax.dynamic_slice_in_dim(exchange, 2 * c, 2, 0)
    kept = kept + lax.ppermute(gone, "c", ring(NC, 1))
    amp_float = amplitudes.astype(jnp.float32)
    amp_kept = lax.dynamic_slice_in_dim(amp_float, 2 * c, 2, 0)
    right = jnp.einsum("pab,pbc->pac", kept, amp_kept, precision=lax.Precision.HIGHEST)
    quadratic = jnp.einsum("pba,pbc->pac", amp_kept, right, precision=lax.Precision.HIGHEST)
    local = kept + quadratic

    own, away = pl.pallas_call(
        couple_kernel,
        out_shape=(
            jax.ShapeDtypeStruct((2, v, v), jnp.float32),
            jax.ShapeDtypeStruct((NX - 1, 2, v, v), jnp.bfloat16),
        ),
        in_specs=[smem] + [vmem] * 6,
        out_specs=(vmem, vmem),
        scratch_shapes=[
            pltpu.VMEM((NX, 8, v), jnp.float32),
            pltpu.VMEM((NX, 8, v), jnp.int32),
            pltpu.SMEM((NX, 8, v), jnp.float32),
            pltpu.SMEM((NX, 8, v), jnp.int32),
            pltpu.SMEM((2, 24), jnp.int32),
            pltpu.VMEM((NX, 2, v, v), jnp.float32),
            pltpu.VMEM((v, v), jnp.bfloat16),
            pltpu.SemaphoreType.DMA((2,)),
        ],
        compiler_params=pltpu.CompilerParams(vmem_limit_bytes=32 * 1024 * 1024),
        name="couple",
    )(where, *x_parts, q_mine, q_other)
    back = [lax.ppermute(away[k - 1], "x", ring(NX, NX - k)) for k in (1, 2, 3)]
    share = local - (own + sum(b.astype(jnp.float32) for b in back))
    y1, y2, y3 = (lax.ppermute(share, "y", ring(NY, k)) for k in (1, 2, 3))
    mine = (share + y2) + (y1 + y3)
    other = lax.ppermute(mine, "c", ring(NC, 1))
    total = jnp.where(
        c == 0, jnp.concatenate([mine, other], axis=0), jnp.concatenate([other, mine], axis=0)
    )
    diagonal = (energies[:, :, None] + energies[:, None, :] - pair_shift[:, None, None]) * amp_float
    inside = jnp.arange(v, dtype=jnp.int32)[None, :] < pno_count[:, None]
    return jnp.where(inside[:, :, None] & inside[:, None, :], total + diagonal, jnp.float32(0.0))


def solution(mesh):
    owners = mesh.devices.shape[0]
    fine = Mesh(mesh.devices.reshape(owners // NX, NX, NY, NC), ("z", "x", "y", "c"))
    pair, aux = ("z", "x"), ("y", "c")
    placed = (
        P(pair, None, None),
        P(pair, None, None),
        P(pair, None),
        P(pair),
        P(pair),
        P(pair, None),
        P(pair, None),
        P(pair, aux, None),
        P(pair, aux, None),
    )
    return jax.shard_map(
        shards, mesh=fine, in_specs=placed, out_specs=P(pair, None, None), check_vma=False
    )
```

```python
import jax
import jax.numpy as jnp
from jax import lax
from jax.experimental import pallas as pl
from jax.experimental.pallas import tpu as pltpu
from jax.sharding import Mesh
from jax.sharding import PartitionSpec as P

NX, NY, NC = 4, 4, 2
META = 16
STEP = 4


def opposite(size, step):
    up = [(i * NC, ((i + step) % size) * NC) for i in range(size)]
    down = [(i * NC + 1, ((i - step) % size) * NC + 1) for i in range(size)]
    return up + down


def ring(size, step):
    return [(i, (i + step) % size) for i in range(size)]


def partners(turn):
    table = ([1, 0, 3, 2], [3, 2, 1, 0])
    return [
        (y * NC + c, table[(turn + c) % 2][y] * NC + c) for y in range(NY) for c in range(NC)
    ]


def prepare_kernel(where, pairs, weights, coef, amp, z_full, x_all, x_own, sem):
    y, c = where[2], where[3]
    _, nv, v = coef.shape
    copies = []

    def fetch(src, dst):
        copy = pltpu.make_async_copy(src, dst, sem.at[len(copies)])
        copy.start()
        copies.append(copy)

    fetch(coef.at[y], z_full.at[pl.ds(0, nv)])
    fetch(amp.at[y], z_full.at[pl.ds(nv, v)])
    for s in range(4):
        fetch(coef.at[s], x_all.at[pl.ds(s * nv, nv)])
    for s in range(2):
        fetch(coef.at[2 * c + s], x_own.at[pl.ds(s * nv, nv)])
    weight = weights[...]
    first = weight.astype(jnp.bfloat16).astype(jnp.float32)
    second = (weight - first).astype(jnp.bfloat16).astype(jnp.float32)
    third = weight - first - second
    meta = jnp.concatenate([pairs[...].astype(jnp.float32), first, second, third], axis=0)
    meta = meta.astype(jnp.bfloat16)
    for ref, start in ((x_all, 4 * nv), (x_own, 2 * nv)):
        ref[start : start + META, :] = jnp.zeros((META, v), jnp.bfloat16)
        ref[start : start + META, : meta.shape[1]] = meta
    for copy in copies:
        copy.wait()


def pack_kernel(where, first, second, after, packed):
    c = where[3]
    rows, v = first.shape
    nv = rows - v
    half, amp_half = nv // NC, v // NC
    packed[:rows, :] = first[...]
    packed[rows : rows + half, :] = second[pl.ds(pl.multiple_of(c * half, half), half), :]
    packed[rows + half :, :] = second[
        pl.ds(pl.multiple_of(nv + c * amp_half, amp_half), amp_half), :
    ]


def turn_kernel(near, own, turned):
    nv = turned.shape[1]
    v = near.shape[1]
    at = 0
    for ref, slots in ((near, 4), (own, 2)):
        for s in range(slots):
            turned[at * v : (at + 1) * v, :] = ref[s * nv : (s + 1) * nv, :].T
            at += 1


def couple_kernel(where, turned, x_near, x_far, x_own, z_full, *refs):
    z, x, y, c = where[0], where[1], where[2], where[3]
    mine, other = refs[:3], refs[3:6]
    near, far, own, left, right, q, acc, meta, meta_f, meta_i, sm_f, sm_i, picks, factors, sem = refs[6:]
    nz, rows, v = q.shape
    nv = rows - v
    half, amp_half = nv // NC, v // NC
    copies = []

    def fetch(src, dst):
        copy = pltpu.make_async_copy(src, dst, sem.at[len(copies)])
        copy.start()
        copies.append(copy)

    fetch(x_near.at[pl.ds(4 * nv, META)], meta.at[0])
    fetch(x_own.at[pl.ds(2 * nv, META)], meta.at[1])
    fetch(x_far, right)
    early = list(copies)
    fetch(turned, left.at[pl.ds(0, 6 * v)])
    fetch(z_full, q.at[z])
    sign = 1 - 2 * c
    across = lax.rem(z + 4, nz)
    for refs_from, away, part in ((mine, -sign, c), (other, sign, 1 - c)):
        for k in range(1, 4):
            src = refs_from[k - 1].at[pl.ds(0, rows)] if k == 3 else refs_from[k - 1]
            fetch(src, q.at[lax.rem(z + away * k + nz, nz)])
        fetch(
            refs_from[2].at[pl.ds(rows, half)],
            q.at[across, pl.ds(pl.multiple_of(part * half, half), half)],
        )
        fetch(
            refs_from[2].at[pl.ds(rows + half, amp_half)],
            q.at[across, pl.ds(pl.multiple_of(nv + part * amp_half, amp_half), amp_half)],
        )
    for copy in early:
        copy.wait()
    for i, block in enumerate((meta[0], meta[1], right[2 * nv :, :])):
        block = block.astype(jnp.float32)
        meta_i[i, :4] = block[:4].astype(jnp.int32)
        meta_f[i, :4] = block[4:8] + block[8:12] + block[12:16]
    copy_f = pltpu.make_async_copy(meta_f, sm_f, sem.at[0])
    copy_i = pltpu.make_async_copy(meta_i, sm_i, sem.at[1])
    copy_f.start()
    copy_i.start()
    for s in range(2):
        left[(6 + s) * v : (7 + s) * v, :] = right[s * nv : (s + 1) * nv, :].T
    copy_f.wait()
    copy_i.wait()
    found = 0
    wanted = x * 4 + y
    for p in range(8):
        source = 0 if p < 4 else 1 if p < 6 else 2
        slot = p if p < 4 else 2 * c + p % 2
        for k in range(16):
            pair_id = sm_i[source, slot, k]
            picks[found] = pair_id * 8 + p
            factors[found] = sm_f[source, slot, k]
            found += (pair_id % 16 == wanted).astype(jnp.int32)
    for j in range(STEP):
        picks[found + j] = 0
        factors[found + j] = 0.0
    acc[...] = jnp.zeros_like(acc)
    for copy in copies[len(early) :]:
        copy.wait()

    def several(i, carry):
        at = [i * STEP + j for j in range(STEP)]
        ps = [picks[a] % 8 for a in at]
        zs = [picks[a] // (8 * 4 * NX) for a in at]
        inter = [
            jnp.dot(
                left[pl.ds(pl.multiple_of(p * v, v), v), :],
                q[zq, :nv, :],
                preferred_element_type=jnp.float32,
            ).astype(jnp.bfloat16)
            for p, zq in zip(ps, zs)
        ]
        mid = [
            jnp.dot(a, q[zq, nv:, :], preferred_element_type=jnp.float32).astype(jnp.bfloat16)
            for a, zq in zip(inter, zs)
        ]
        proj = [
            lax.dot_general(m, a, (((1,), (1,)), ((), ())), preferred_element_type=jnp.float32)
            .astype(jnp.bfloat16)
            .astype(jnp.float32)
            for m, a in zip(mid, inter)
        ]
        for a, p, value in zip(at, ps, proj):
            acc[p] += factors[a] * value
        return carry

    lax.fori_loop(0, (found + STEP - 1) // STEP, several, 0)
    near[...] = acc[:4].astype(jnp.bfloat16)
    own[...] = acc[4:6]
    far[...] = acc[6:8].astype(jnp.bfloat16)


def settle_kernel(where, local, near, far, own, kept, gone):
    c = where[3]
    for s in range(2):
        gone[s] = local[2 * (1 - c) + s] - near[2 * (1 - c) + s].astype(jnp.float32)
        kept[s] = local[2 * c + s] - near[2 * c + s].astype(jnp.float32) - (
            own[s] + far[s].astype(jnp.float32)
        )


def shards(
    amplitudes,
    coefficients,
    energies,
    pair_shift,
    pno_count,
    coupled_pairs,
    coupling_weight,
    slab_one,
    slab_two,
):
    pairs, v, _ = amplitudes.shape
    nv = coefficients.shape[1]
    nz = lax.axis_size("z")
    where = jnp.stack([lax.axis_index(a) for a in ("z", "x", "y", "c")]).astype(jnp.int32)
    c = where[3]
    smem = pl.BlockSpec(memory_space=pltpu.SMEM)
    vmem = pl.BlockSpec(memory_space=pltpu.VMEM)
    anywhere = pl.BlockSpec(memory_space=pl.ANY)
    bf16, f32, i32 = jnp.bfloat16, jnp.float32, jnp.int32

    z_full, x_all, x_own = pl.pallas_call(
        prepare_kernel,
        out_shape=(
            jax.ShapeDtypeStruct((nv + v, v), bf16),
            jax.ShapeDtypeStruct((4 * nv + META, v), bf16),
            jax.ShapeDtypeStruct((2 * nv + META, v), bf16),
        ),
        in_specs=[smem, vmem, vmem, anywhere, anywhere],
        out_specs=(vmem,) * 3,
        scratch_shapes=[pltpu.SemaphoreType.DMA((8,))],
        compiler_params=pltpu.CompilerParams(vmem_limit_bytes=4 * 1024 * 1024),
        name="prepare",
    )(where, coupled_pairs, coupling_weight, coefficients, amplitudes)

    swap = ring(NC, 1)
    z_one = lax.ppermute(z_full, ("z", "c"), opposite(nz, 1))
    z_two = lax.ppermute(z_full, ("z", "c"), opposite(nz, 2))
    x_near = lax.ppermute(x_all, ("x", "c"), opposite(NX, 1))
    x_far = lax.ppermute(x_own, "x", ring(NX, 2))
    exchange = jnp.einsum("pqa,pqb->pab", slab_one, slab_two, preferred_element_type=f32)
    amp_float = amplitudes.astype(f32)
    right = jnp.einsum("pab,pbc->pac", exchange, amp_float, precision=lax.Precision.HIGHEST)
    quadratic = jnp.einsum("pba,pbc->pac", amp_float, right, precision=lax.Precision.HIGHEST)
    local = exchange + quadratic

    z_rest = pl.pallas_call(
        pack_kernel,
        out_shape=jax.ShapeDtypeStruct((nv + v + (nv + v) // NC, v), bf16),
        in_specs=[smem, vmem, vmem, anywhere],
        out_specs=vmem,
        compiler_params=pltpu.CompilerParams(vmem_limit_bytes=4 * 1024 * 1024),
        name="pack",
    )(where, z_one, z_two, exchange)
    z_rest = lax.ppermute(z_rest, ("z", "c"), opposite(nz, 2))
    z_mine = [z_one, z_two, z_rest]
    z_other = [lax.ppermute(b, "c", swap) for b in z_mine]

    turned = pl.pallas_call(
        turn_kernel,
        out_shape=jax.ShapeDtypeStruct((6 * v, nv), bf16),
        in_specs=[vmem, vmem],
        out_specs=vmem,
        compiler_params=pltpu.CompilerParams(vmem_limit_bytes=6 * 1024 * 1024),
        cost_estimate=pl.CostEstimate(flops=0, bytes_accessed=12_000_000, transcendentals=0),
        name="turn",
    )(x_near, x_own)
    near, far, own = pl.pallas_call(
        couple_kernel,
        out_shape=(
            jax.ShapeDtypeStruct((4, v, v), bf16),
            jax.ShapeDtypeStruct((2, v, v), bf16),
            jax.ShapeDtypeStruct((2, v, v), f32),
        ),
        in_specs=[smem] + [anywhere] * 11,
        out_specs=(vmem, vmem, vmem),
        scratch_shapes=[
            pltpu.VMEM((8 * v, nv), bf16),
            pltpu.VMEM((2 * nv + META, v), bf16),
            pltpu.VMEM((nz, nv + v, v), bf16),
            pltpu.VMEM((8, v, v), f32),
            pltpu.VMEM((2, META, v), bf16),
            pltpu.VMEM((3, 8, v), f32),
            pltpu.VMEM((3, 8, v), i32),
            pltpu.SMEM((3, 8, v), f32),
            pltpu.SMEM((3, 8, v), i32),
            pltpu.SMEM((128 + STEP,), i32),
            pltpu.SMEM((128 + STEP,), f32),
            pltpu.SemaphoreType.DMA((16,)),
        ],
        compiler_params=pltpu.CompilerParams(vmem_limit_bytes=8 * 1024 * 1024),
        cost_estimate=pl.CostEstimate(flops=0, bytes_accessed=12_000_000, transcendentals=0),
        name="couple",
    )(where, turned, x_near, x_far, x_own, z_full, *z_mine, *z_other)

    near_back = lax.ppermute(near, ("x", "c"), opposite(NX, NX - 1))
    far_back = lax.ppermute(far, "x", ring(NX, 2))
    kept, gone = pl.pallas_call(
        settle_kernel,
        out_shape=(jax.ShapeDtypeStruct((2, v, v), f32),) * 2,
        in_specs=[smem] + [vmem] * 4,
        out_specs=(vmem, vmem),
        compiler_params=pltpu.CompilerParams(vmem_limit_bytes=4 * 1024 * 1024),
        name="settle",
    )(where, local, near_back, far_back, own)
    share = kept + lax.ppermute(gone, "c", swap)
    share = share + lax.ppermute(share, ("y", "c"), partners(0))
    share = share + lax.ppermute(share, ("y", "c"), partners(1))
    other = lax.ppermute(share, "c", swap)
    total = jnp.where(
        c == 0, jnp.concatenate([share, other], axis=0), jnp.concatenate([other, share], axis=0)
    )
    diagonal = (energies[:, :, None] + energies[:, None, :] - pair_shift[:, None, None]) * amp_float
    inside = jnp.arange(v, dtype=i32)[None, :] < pno_count[:, None]
    return jnp.where(inside[:, :, None] & inside[:, None, :], total + diagonal, f32(0.0))


def solution(mesh):
    owners = mesh.devices.shape[0]
    fine = Mesh(mesh.devices.reshape(owners // NX, NX, NY, NC), ("z", "x", "y", "c"))
    pair, aux = ("z", "x"), ("y", "c")
    placed = (
        P(pair, None, None),
        P(pair, None, None),
        P(pair, None),
        P(pair),
        P(pair),
        P(pair, None),
        P(pair, None),
        P(pair, aux, None),
        P(pair, aux, None),
    )
    return jax.shard_map(
        shards, mesh=fine, in_specs=placed, out_specs=P(pair, None, None), check_vma=False
    )
```

```python
import jax
import jax.numpy as jnp
from jax import lax
from jax.experimental import pallas as pl
from jax.experimental.pallas import tpu as pltpu
from jax.sharding import Mesh
from jax.sharding import PartitionSpec as P

NX, NY, NC = 4, 4, 2
META = 16
STEP = 4


def opposite(size, step):
    up = [(i * NC, ((i + step) % size) * NC) for i in range(size)]
    down = [(i * NC + 1, ((i - step) % size) * NC + 1) for i in range(size)]
    return up + down


def ring(size, step):
    return [(i, (i + step) % size) for i in range(size)]


def partners(turn):
    table = ([1, 0, 3, 2], [3, 2, 1, 0])
    return [
        (y * NC + c, table[(turn + c) % 2][y] * NC + c) for y in range(NY) for c in range(NC)
    ]


def prepare_kernel(pairs, weights, coef, amp, z_full, x_all, x_own, pairs_v, weights_v, sem):
    y, c = lax.axis_index("y"), lax.axis_index("c")
    _, nv, v = coef.shape
    copies = []

    def fetch(src, dst):
        copy = pltpu.make_async_copy(src, dst, sem.at[len(copies)])
        copy.start()
        copies.append(copy)

    fetch(pairs, pairs_v)
    fetch(weights, weights_v)
    at = 0
    for part in range(NC):
        for ref, size in ((coef, nv // NC), (amp, v // NC)):
            fetch(ref.at[y, pl.ds(part * size, size)], z_full.at[pl.ds(at, size)])
            at += size
    for s in range(4):
        fetch(coef.at[s], x_all.at[pl.ds(s * nv, nv)])
    for s in range(2):
        fetch(coef.at[2 * c + s], x_own.at[pl.ds(s * nv, nv)])
    copies[0].wait()
    copies[1].wait()
    weight = weights_v[...]
    first = weight.astype(jnp.bfloat16).astype(jnp.float32)
    second = (weight - first).astype(jnp.bfloat16).astype(jnp.float32)
    third = weight - first - second
    meta = jnp.concatenate([pairs_v[...].astype(jnp.float32), first, second, third], axis=0)
    meta = meta.astype(jnp.bfloat16)
    for ref, start in ((x_all, 4 * nv), (x_own, 2 * nv)):
        ref[start : start + META, :] = jnp.zeros((META, v), jnp.bfloat16)
        ref[start : start + META, : meta.shape[1]] = meta
    for copy in copies[2:]:
        copy.wait()


def couple_kernel(where, x_near, x_own, x_far, z_full, *refs):
    z, x, y, c = where[0], where[1], where[2], where[3]
    mine, other = refs[:4], refs[4:8]
    near, far, own, left, q, acc, meta_f, meta_i, sm_f, sm_i, codes, sem = refs[8:]
    nz, rows, v = q.shape
    nv = rows - v
    half, amp_half = nv // NC, v // NC
    sources = ((x_near, 4), (x_own, 2), (x_far, 2))
    for i, (ref, slots) in enumerate(sources):
        block = ref[slots * nv : slots * nv + META, :].astype(jnp.float32)
        meta_i[4 * i : 4 * i + 4, :] = block[:4].astype(jnp.int32)
        meta_f[4 * i : 4 * i + 4, :] = block[4:8] + block[8:12] + block[12:16]
    copy_i = pltpu.make_async_copy(meta_i, sm_i, sem.at[0])
    copy_f = pltpu.make_async_copy(meta_f, sm_f, sem.at[1])
    copy_i.start()
    copy_f.start()
    at = 0
    for ref, slots in sources:
        for s in range(slots):
            left[at * v : (at + 1) * v, :] = ref[s * nv : (s + 1) * nv, :].T
            at += 1
    acc[...] = jnp.zeros_like(acc)
    sign = 1 - 2 * c
    across = lax.rem(z + 4, nz)
    step = half + amp_half

    def place(at, part, block):
        q[at, pl.ds(pl.multiple_of(part * half, half), half), :] = block[:half]
        q[at, pl.ds(pl.multiple_of(nv + part * amp_half, amp_half), amp_half), :] = block[half:]

    for part in range(NC):
        lower = slice(part * step, (part + 1) * step)
        place(z, part, z_full[lower, :])
        for blocks, away in ((mine, -sign), (other, sign)):
            for k in range(1, 4):
                place(lax.rem(z + away * k + nz, nz), part, blocks[k - 1][lower, :])
    place(across, c, mine[3][...])
    place(across, 1 - c, other[3][...])
    copy_i.wait()
    copy_f.wait()
    found = 0
    wanted = x * 4 + y
    for p in range(8):
        row = p if p < 4 else 4 * (p // 2 - 1) + 2 * c + p % 2
        base = row * 128 + p * 16
        ids = [sm_i[row, k] for k in range(16)]
        values = [
            lax.shift_left(lax.shift_right_logical(n, 4), 11) + (base + k)
            for k, n in enumerate(ids)
        ]
        hits = [jnp.where((n & 15) == wanted, 1, 0) for n in ids]
        for value, hit in zip(values, hits):
            codes[found] = value
            found = found + hit
    for j in range(STEP - 1):
        codes[found + j] = -1

    def several(i, carry):
        code = [codes[i * STEP + j] for j in range(STEP)]
        used = [jnp.where(n >= 0, 1.0, 0.0) for n in code]
        code = [jnp.maximum(n, 0) for n in code]
        ps = [lax.shift_right_logical(n, 4) & 7 for n in code]
        zs = [lax.shift_right_logical(n, 11) for n in code]
        weights = [sm_f[lax.shift_right_logical(n, 7) & 15, n & 15] * u for n, u in zip(code, used)]
        inter = [
            jnp.dot(
                left[pl.ds(pl.multiple_of(p * v, v), v), :],
                q[zq, :nv, :],
                preferred_element_type=jnp.float32,
            ).astype(jnp.bfloat16)
            for p, zq in zip(ps, zs)
        ]
        mid = [
            jnp.dot(a, q[zq, nv:, :], preferred_element_type=jnp.float32).astype(jnp.bfloat16)
            for a, zq in zip(inter, zs)
        ]
        proj = [
            lax.dot_general(m, a, (((1,), (1,)), ((), ())), preferred_element_type=jnp.float32)
            .astype(jnp.bfloat16)
            .astype(jnp.float32)
            for m, a in zip(mid, inter)
        ]
        for weight, p, value in zip(weights, ps, proj):
            acc[p] += weight * value
        return carry

    lax.fori_loop(0, (found + STEP - 1) // STEP, several, 0)
    near[...] = acc[:4].astype(jnp.bfloat16)
    own[...] = acc[4:6]
    far[...] = acc[6:8].astype(jnp.bfloat16)


def settle_kernel(where, local, near, far, own, kept, gone):
    c = where[3]
    for s in range(2):
        gone[s] = local[2 * (1 - c) + s] - near[2 * (1 - c) + s].astype(jnp.float32)
        kept[s] = local[2 * c + s] - near[2 * c + s].astype(jnp.float32) - (
            own[s] + far[s].astype(jnp.float32)
        )


def shards(
    amplitudes,
    coefficients,
    energies,
    pair_shift,
    pno_count,
    coupled_pairs,
    coupling_weight,
    slab_one,
    slab_two,
):
    pairs, v, _ = amplitudes.shape
    nv = coefficients.shape[1]
    nz = lax.axis_size("z")
    where = jnp.stack([lax.axis_index(a) for a in ("z", "x", "y", "c")]).astype(jnp.int32)
    c = where[3]
    smem = pl.BlockSpec(memory_space=pltpu.SMEM)
    vmem = pl.BlockSpec(memory_space=pltpu.VMEM)
    anywhere = pl.BlockSpec(memory_space=pl.ANY)
    bf16, f32, i32 = jnp.bfloat16, jnp.float32, jnp.int32

    small = pltpu.CompilerParams(vmem_limit_bytes=4 * 1024 * 1024)
    half, amp_half = nv // NC, v // NC
    z_full, x_all, x_own = pl.pallas_call(
        prepare_kernel,
        out_shape=(
            jax.ShapeDtypeStruct((nv + v, v), bf16),
            jax.ShapeDtypeStruct((4 * nv + META, v), bf16),
            jax.ShapeDtypeStruct((2 * nv + META, v), bf16),
        ),
        in_specs=[anywhere] * 4,
        out_specs=(vmem,) * 3,
        scratch_shapes=[
            pltpu.VMEM(coupled_pairs.shape, i32),
            pltpu.VMEM(coupling_weight.shape, f32),
            pltpu.SemaphoreType.DMA((12,)),
        ],
        compiler_params=pltpu.CompilerParams(vmem_limit_bytes=62 * 1024 * 1024),
        name="prepare",
    )(coupled_pairs, coupling_weight, coefficients, amplitudes)

    swap = ring(NC, 1)
    z_one = lax.ppermute(z_full, ("z", "c"), opposite(nz, 1))
    z_two = lax.ppermute(z_full, ("z", "c"), opposite(nz, 2))
    x_near = lax.ppermute(x_all, ("x", "c"), opposite(NX, 1))
    x_far = lax.ppermute(x_own, "x", ring(NX, 2))

    exchange = jnp.einsum("pqa,pqb->pab", slab_one, slab_two, preferred_element_type=f32)
    amp_float = amplitudes.astype(f32)
    right = jnp.einsum("pab,pbc->pac", exchange, amp_float, precision=lax.Precision.HIGHEST)
    quadratic = jnp.einsum("pba,pbc->pac", amp_float, right, precision=lax.Precision.HIGHEST)
    local = exchange + quadratic

    z_three = lax.ppermute(z_two, ("z", "c"), opposite(nz, 1))
    z_four = lax.dynamic_slice_in_dim(z_two, c * (half + amp_half), half + amp_half, 0)
    z_four = lax.ppermute(z_four, ("z", "c"), opposite(nz, 2))
    z_mine = [z_one, z_two, z_three, z_four]
    z_other = [lax.ppermute(b, "c", swap) for b in z_mine]

    near, far, own = pl.pallas_call(
        couple_kernel,
        out_shape=(
            jax.ShapeDtypeStruct((4, v, v), bf16),
            jax.ShapeDtypeStruct((2, v, v), bf16),
            jax.ShapeDtypeStruct((2, v, v), f32),
        ),
        in_specs=[smem] + [vmem] * 12,
        out_specs=(vmem, vmem, vmem),
        scratch_shapes=[
            pltpu.VMEM((8 * v, nv), bf16),
            pltpu.VMEM((nz, nv + v, v), bf16),
            pltpu.VMEM((8, v, v), f32),
            pltpu.VMEM((16, v), f32),
            pltpu.VMEM((16, v), i32),
            pltpu.SMEM((16, v), f32),
            pltpu.SMEM((16, v), i32),
            pltpu.SMEM((136,), i32),
            pltpu.SemaphoreType.DMA((2,)),
        ],
        compiler_params=pltpu.CompilerParams(vmem_limit_bytes=8 * 1024 * 1024),
        cost_estimate=pl.CostEstimate(flops=0, bytes_accessed=12_000_000, transcendentals=0),
        name="couple",
    )(where, x_near, x_own, x_far, z_full, *z_mine, *z_other)

    near_back = lax.ppermute(near, ("x", "c"), opposite(NX, NX - 1))
    far_back = lax.ppermute(far, "x", ring(NX, 2))
    kept, gone = pl.pallas_call(
        settle_kernel,
        out_shape=(jax.ShapeDtypeStruct((2, v, v), f32),) * 2,
        in_specs=[smem] + [vmem] * 4,
        out_specs=(vmem, vmem),
        compiler_params=pltpu.CompilerParams(vmem_limit_bytes=4 * 1024 * 1024),
        name="settle",
    )(where, local, near_back, far_back, own)
    share = kept + lax.ppermute(gone, "c", swap)
    share = share + lax.ppermute(share, ("y", "c"), partners(0))
    share = share + lax.ppermute(share, ("y", "c"), partners(1))
    other = lax.ppermute(share, "c", swap)
    total = jnp.where(
        c == 0, jnp.concatenate([share, other], axis=0), jnp.concatenate([other, share], axis=0)
    )
    diagonal = (energies[:, :, None] + energies[:, None, :] - pair_shift[:, None, None]) * amp_float
    inside = jnp.arange(v, dtype=i32)[None, :] < pno_count[:, None]
    return jnp.where(inside[:, :, None] & inside[:, None, :], total + diagonal, f32(0.0))


def solution(mesh):
    owners = mesh.devices.shape[0]
    fine = Mesh(mesh.devices.reshape(owners // NX, NX, NY, NC), ("z", "x", "y", "c"))
    pair, aux = ("z", "x"), ("y", "c")
    placed = (
        P(pair, None, None),
        P(pair, None, None),
        P(pair, None),
        P(pair),
        P(pair),
        P(pair, None),
        P(pair, None),
        P(pair, aux, None),
        P(pair, aux, None),
    )
    return jax.shard_map(
        shards, mesh=fine, in_specs=placed, out_specs=P(pair, None, None), check_vma=False
    )
```

```python
import jax
import jax.numpy as jnp
from jax import lax
from jax.experimental import pallas as pl
from jax.experimental.pallas import tpu as pltpu
from jax.sharding import Mesh
from jax.sharding import PartitionSpec as P

NX, NY, NC = 4, 4, 2
META = 16
STEP = 4


def opposite(size, step):
    up = [(i * NC, ((i + step) % size) * NC) for i in range(size)]
    down = [(i * NC + 1, ((i - step) % size) * NC + 1) for i in range(size)]
    return up + down


def ring(size, step):
    return [(i, (i + step) % size) for i in range(size)]


def partners(turn):
    table = ([1, 0, 3, 2], [3, 2, 1, 0])
    return [
        (y * NC + c, table[(turn + c) % 2][y] * NC + c) for y in range(NY) for c in range(NC)
    ]


def prepare_kernel(pairs, weights, coef, amp, z_full, x_all, x_own, pairs_v, weights_v, sem):
    y, c = lax.axis_index("y"), lax.axis_index("c")
    _, nv, v = coef.shape
    copies = []

    def fetch(src, dst):
        copy = pltpu.make_async_copy(src, dst, sem.at[len(copies)])
        copy.start()
        copies.append(copy)

    fetch(pairs, pairs_v)
    fetch(weights, weights_v)
    at = 0
    for part in range(NC):
        for ref, size in ((coef, nv // NC), (amp, v // NC)):
            fetch(ref.at[y, pl.ds(part * size, size)], z_full.at[pl.ds(at, size)])
            at += size
    for s in range(4):
        fetch(coef.at[s], x_all.at[pl.ds(s * nv, nv)])
    for s in range(2):
        fetch(coef.at[2 * c + s], x_own.at[pl.ds(s * nv, nv)])
    copies[0].wait()
    copies[1].wait()
    weight = weights_v[...]
    first = weight.astype(jnp.bfloat16).astype(jnp.float32)
    second = (weight - first).astype(jnp.bfloat16).astype(jnp.float32)
    third = weight - first - second
    meta = jnp.concatenate([pairs_v[...].astype(jnp.float32), first, second, third], axis=0)
    meta = meta.astype(jnp.bfloat16)
    for ref, start in ((x_all, 4 * nv), (x_own, 2 * nv)):
        ref[start : start + META, :] = jnp.zeros((META, v), jnp.bfloat16)
        ref[start : start + META, : meta.shape[1]] = meta
    for copy in copies[2:]:
        copy.wait()


def couple_kernel(where, x_near, x_own, x_far, z_full, *refs):
    z, x, y, c = where[0], where[1], where[2], where[3]
    mine, other = refs[:4], refs[4:8]
    near, far, own, left, q, acc, meta_f, meta_i, sm_f, sm_i, codes, sem = refs[8:]
    nz, rows, v = q.shape
    nv = rows - v
    half, amp_half = nv // NC, v // NC
    sources = ((x_near, 4), (x_own, 2), (x_far, 2))
    for i, (ref, slots) in enumerate(sources):
        block = ref[slots * nv : slots * nv + META, :].astype(jnp.float32)
        meta_i[4 * i : 4 * i + 4, :] = block[:4].astype(jnp.int32)
        meta_f[4 * i : 4 * i + 4, :] = block[4:8] + block[8:12] + block[12:16]
    copy_i = pltpu.make_async_copy(meta_i, sm_i, sem.at[0])
    copy_f = pltpu.make_async_copy(meta_f, sm_f, sem.at[1])
    copy_i.start()
    copy_f.start()
    at = 0
    for ref, slots in sources:
        for s in range(slots):
            left[at * v : (at + 1) * v, :] = ref[s * nv : (s + 1) * nv, :].T
            at += 1
    acc[...] = jnp.zeros_like(acc)
    sign = 1 - 2 * c
    across = lax.rem(z + 4, nz)
    step = half + amp_half

    def place(at, part, block):
        q[at, pl.ds(pl.multiple_of(part * half, half), half), :] = block[:half]
        q[at, pl.ds(pl.multiple_of(nv + part * amp_half, amp_half), amp_half), :] = block[half:]

    for part in range(NC):
        lower = slice(part * step, (part + 1) * step)
        place(z, part, z_full[lower, :])
        for blocks, away in ((mine, -sign), (other, sign)):
            for k in range(1, 4):
                place(lax.rem(z + away * k + nz, nz), part, blocks[k - 1][lower, :])
    place(across, c, mine[3][...])
    place(across, 1 - c, other[3][...])
    copy_i.wait()
    copy_f.wait()
    found = 0
    wanted = x * 4 + y
    for p in range(8):
        row = p if p < 4 else 4 * (p // 2 - 1) + 2 * c + p % 2
        base = row * 128 + p * 16
        ids = [sm_i[row, k] for k in range(16)]
        values = [
            lax.shift_left(lax.shift_right_logical(n, 4), 11) + (base + k)
            for k, n in enumerate(ids)
        ]
        hits = [jnp.where((n & 15) == wanted, 1, 0) for n in ids]
        for value, hit in zip(values, hits):
            codes[found] = value
            found = found + hit
    for j in range(STEP - 1):
        codes[found + j] = -1

    def several(i, carry):
        code = [codes[i * STEP + j] for j in range(STEP)]
        used = [jnp.where(n >= 0, 1.0, 0.0) for n in code]
        code = [jnp.maximum(n, 0) for n in code]
        ps = [lax.shift_right_logical(n, 4) & 7 for n in code]
        zs = [lax.shift_right_logical(n, 11) for n in code]
        weights = [sm_f[lax.shift_right_logical(n, 7) & 15, n & 15] * u for n, u in zip(code, used)]
        inter = [
            jnp.dot(
                left[pl.ds(pl.multiple_of(p * v, v), v), :],
                q[zq, :nv, :],
                preferred_element_type=jnp.float32,
            ).astype(jnp.bfloat16)
            for p, zq in zip(ps, zs)
        ]
        mid = [
            jnp.dot(a, q[zq, nv:, :], preferred_element_type=jnp.float32).astype(jnp.bfloat16)
            for a, zq in zip(inter, zs)
        ]
        proj = [
            lax.dot_general(m, a, (((1,), (1,)), ((), ())), preferred_element_type=jnp.float32)
            .astype(jnp.bfloat16)
            .astype(jnp.float32)
            for m, a in zip(mid, inter)
        ]
        for weight, p, value in zip(weights, ps, proj):
            acc[p] += weight * value
        return carry

    lax.fori_loop(0, (found + STEP - 1) // STEP, several, 0)
    near[...] = acc[:4].astype(jnp.bfloat16)
    own[...] = acc[4:6]
    far[...] = acc[6:8].astype(jnp.bfloat16)


def settle_kernel(where, local, near, far, own, kept, gone):
    c = where[3]
    for s in range(2):
        gone[s] = local[2 * (1 - c) + s] - near[2 * (1 - c) + s].astype(jnp.float32)
        kept[s] = local[2 * c + s] - near[2 * c + s].astype(jnp.float32) - (
            own[s] + far[s].astype(jnp.float32)
        )


def shards(
    amplitudes,
    coefficients,
    energies,
    pair_shift,
    pno_count,
    coupled_pairs,
    coupling_weight,
    slab_one,
    slab_two,
):
    pairs, v, _ = amplitudes.shape
    nv = coefficients.shape[1]
    nz = lax.axis_size("z")
    where = jnp.stack([lax.axis_index(a) for a in ("z", "x", "y", "c")]).astype(jnp.int32)
    c = where[3]
    smem = pl.BlockSpec(memory_space=pltpu.SMEM)
    vmem = pl.BlockSpec(memory_space=pltpu.VMEM)
    anywhere = pl.BlockSpec(memory_space=pl.ANY)
    bf16, f32, i32 = jnp.bfloat16, jnp.float32, jnp.int32

    small = pltpu.CompilerParams(vmem_limit_bytes=4 * 1024 * 1024)
    half, amp_half = nv // NC, v // NC
    z_full, x_all, x_own = pl.pallas_call(
        prepare_kernel,
        out_shape=(
            jax.ShapeDtypeStruct((nv + v, v), bf16),
            jax.ShapeDtypeStruct((4 * nv + META, v), bf16),
            jax.ShapeDtypeStruct((2 * nv + META, v), bf16),
        ),
        in_specs=[anywhere] * 4,
        out_specs=(vmem,) * 3,
        scratch_shapes=[
            pltpu.VMEM(coupled_pairs.shape, i32),
            pltpu.VMEM(coupling_weight.shape, f32),
            pltpu.SemaphoreType.DMA((12,)),
        ],
        compiler_params=pltpu.CompilerParams(vmem_limit_bytes=62 * 1024 * 1024),
        name="prepare",
    )(coupled_pairs, coupling_weight, coefficients, amplitudes)

    swap = ring(NC, 1)
    z_one = lax.ppermute(z_full, ("z", "c"), opposite(nz, 1))
    z_two = lax.ppermute(z_full, ("z", "c"), opposite(nz, 2))
    x_near = lax.ppermute(x_all, ("x", "c"), opposite(NX, 1))
    x_far = lax.ppermute(x_own, "x", ring(NX, 2))

    slab_one, slab_two, _ = lax.optimization_barrier((slab_one, slab_two, z_two))
    exchange = jnp.einsum("pqa,pqb->pab", slab_one, slab_two, preferred_element_type=f32)
    amp_float = amplitudes.astype(f32)
    right = jnp.einsum("pab,pbc->pac", exchange, amp_float, precision=lax.Precision.HIGHEST)
    quadratic = jnp.einsum("pba,pbc->pac", amp_float, right, precision=lax.Precision.HIGHEST)
    local = exchange + quadratic

    z_three = lax.ppermute(z_two, ("z", "c"), opposite(nz, 1))
    z_four = lax.dynamic_slice_in_dim(z_two, c * (half + amp_half), half + amp_half, 0)
    z_four = lax.ppermute(z_four, ("z", "c"), opposite(nz, 2))
    z_mine = [z_one, z_two, z_three, z_four]
    z_other = [lax.ppermute(b, "c", swap) for b in z_mine]

    near, far, own = pl.pallas_call(
        couple_kernel,
        out_shape=(
            jax.ShapeDtypeStruct((4, v, v), bf16),
            jax.ShapeDtypeStruct((2, v, v), bf16),
            jax.ShapeDtypeStruct((2, v, v), f32),
        ),
        in_specs=[smem] + [vmem] * 12,
        out_specs=(vmem, vmem, vmem),
        scratch_shapes=[
            pltpu.VMEM((8 * v, nv), bf16),
            pltpu.VMEM((nz, nv + v, v), bf16),
            pltpu.VMEM((8, v, v), f32),
            pltpu.VMEM((16, v), f32),
            pltpu.VMEM((16, v), i32),
            pltpu.SMEM((16, v), f32),
            pltpu.SMEM((16, v), i32),
            pltpu.SMEM((136,), i32),
            pltpu.SemaphoreType.DMA((2,)),
        ],
        compiler_params=pltpu.CompilerParams(vmem_limit_bytes=8 * 1024 * 1024),
        cost_estimate=pl.CostEstimate(flops=0, bytes_accessed=12_000_000, transcendentals=0),
        name="couple",
    )(where, x_near, x_own, x_far, z_full, *z_mine, *z_other)

    near_back = lax.ppermute(near, ("x", "c"), opposite(NX, NX - 1))
    far_back = lax.ppermute(far, "x", ring(NX, 2))
    kept, gone = pl.pallas_call(
        settle_kernel,
        out_shape=(jax.ShapeDtypeStruct((2, v, v), f32),) * 2,
        in_specs=[smem] + [vmem] * 4,
        out_specs=(vmem, vmem),
        compiler_params=pltpu.CompilerParams(vmem_limit_bytes=4 * 1024 * 1024),
        name="settle",
    )(where, local, near_back, far_back, own)
    share = kept + lax.ppermute(gone, "c", swap)
    share = share + lax.ppermute(share, ("y", "c"), partners(0))
    share = share + lax.ppermute(share, ("y", "c"), partners(1))
    other = lax.ppermute(share, "c", swap)
    total = jnp.where(
        c == 0, jnp.concatenate([share, other], axis=0), jnp.concatenate([other, share], axis=0)
    )
    diagonal = (energies[:, :, None] + energies[:, None, :] - pair_shift[:, None, None]) * amp_float
    inside = jnp.arange(v, dtype=i32)[None, :] < pno_count[:, None]
    return jnp.where(inside[:, :, None] & inside[:, None, :], total + diagonal, f32(0.0))


def solution(mesh):
    owners = mesh.devices.shape[0]
    fine = Mesh(mesh.devices.reshape(owners // NX, NX, NY, NC), ("z", "x", "y", "c"))
    pair, aux = ("z", "x"), ("y", "c")
    placed = (
        P(pair, None, None),
        P(pair, None, None),
        P(pair, None),
        P(pair),
        P(pair),
        P(pair, None),
        P(pair, None),
        P(pair, aux, None),
        P(pair, aux, None),
    )
    return jax.shard_map(
        shards, mesh=fine, in_specs=placed, out_specs=P(pair, None, None), check_vma=False
    )
```

```python
import jax
import jax.numpy as jnp
from jax import lax
from jax.experimental import pallas as pl
from jax.experimental.pallas import tpu as pltpu
from jax.sharding import Mesh
from jax.sharding import PartitionSpec as P

NX, NY, NC = 4, 4, 2
META = 16
STEP = 4


def opposite(size, step):
    up = [(i * NC, ((i + step) % size) * NC) for i in range(size)]
    down = [(i * NC + 1, ((i - step) % size) * NC + 1) for i in range(size)]
    return up + down


def ring(size, step):
    return [(i, (i + step) % size) for i in range(size)]


def partners(turn):
    table = ([1, 0, 3, 2], [3, 2, 1, 0])
    return [
        (y * NC + c, table[(turn + c) % 2][y] * NC + c) for y in range(NY) for c in range(NC)
    ]


def prepare_kernel(pairs, weights, coef, amp, z_full, x_all, x_own, pairs_v, weights_v, sem):
    y, c = lax.axis_index("y"), lax.axis_index("c")
    _, nv, v = coef.shape
    copies = []

    def fetch(src, dst):
        copy = pltpu.make_async_copy(src, dst, sem.at[len(copies)])
        copy.start()
        copies.append(copy)

    fetch(pairs, pairs_v)
    fetch(weights, weights_v)
    half, amp_half = nv // NC, v // NC
    step = half + amp_half
    for part in range(NC):
        src = amp.at[y, pl.ds(part * amp_half, amp_half)]
        fetch(src, z_full.at[pl.ds(part * step + half, amp_half)])
    for s in range(4):
        fetch(coef.at[s], x_all.at[pl.ds(s * nv, nv)])
    copies[0].wait()
    copies[1].wait()
    weight = weights_v[...]
    first = weight.astype(jnp.bfloat16).astype(jnp.float32)
    second = (weight - first).astype(jnp.bfloat16).astype(jnp.float32)
    third = weight - first - second
    meta = jnp.concatenate([pairs_v[...].astype(jnp.float32), first, second, third], axis=0)
    meta = meta.astype(jnp.bfloat16)
    for ref, start in ((x_all, 4 * nv), (x_own, 2 * nv)):
        ref[start : start + META, :] = jnp.zeros((META, v), jnp.bfloat16)
        ref[start : start + META, : meta.shape[1]] = meta
    for copy in copies[2:]:
        copy.wait()
    for part in range(NC):
        start = pl.multiple_of(y * nv + part * half, half)
        z_full[part * step : part * step + half, :] = x_all[pl.ds(start, half), :]
    x_own[: 2 * nv, :] = x_all[pl.ds(pl.multiple_of(2 * c * nv, nv), 2 * nv), :]


def couple_kernel(where, x_near, x_own, x_far, z_full, *refs):
    z, x, y, c = where[0], where[1], where[2], where[3]
    mine, other = refs[:4], refs[4:8]
    near, far, own, left, q, acc, meta_f, meta_i, sm_f, sm_i, codes, sem = refs[8:]
    nz, rows, v = q.shape
    nv = rows - v
    half, amp_half = nv // NC, v // NC
    sources = ((x_near, 4), (x_own, 2), (x_far, 2))
    for i, (ref, slots) in enumerate(sources):
        block = ref[slots * nv : slots * nv + META, :].astype(jnp.float32)
        meta_i[4 * i : 4 * i + 4, :] = block[:4].astype(jnp.int32)
        meta_f[4 * i : 4 * i + 4, :] = block[4:8] + block[8:12] + block[12:16]
    copy_i = pltpu.make_async_copy(meta_i, sm_i, sem.at[0])
    copy_f = pltpu.make_async_copy(meta_f, sm_f, sem.at[1])
    copy_i.start()
    copy_f.start()
    at = 0
    for ref, slots in sources:
        for s in range(slots):
            left[at * v : (at + 1) * v, :] = ref[s * nv : (s + 1) * nv, :].T
            at += 1
    acc[...] = jnp.zeros_like(acc)
    sign = 1 - 2 * c
    across = lax.rem(z + 4, nz)
    step = half + amp_half

    def place(at, part, block):
        q[at, pl.ds(pl.multiple_of(part * half, half), half), :] = block[:half]
        q[at, pl.ds(pl.multiple_of(nv + part * amp_half, amp_half), amp_half), :] = block[half:]

    for part in range(NC):
        lower = slice(part * step, (part + 1) * step)
        place(z, part, z_full[lower, :])
        for blocks, away in ((mine, -sign), (other, sign)):
            for k in range(1, 4):
                place(lax.rem(z + away * k + nz, nz), part, blocks[k - 1][lower, :])
    place(across, c, mine[3][...])
    place(across, 1 - c, other[3][...])
    copy_i.wait()
    copy_f.wait()
    found = 0
    wanted = x * 4 + y
    for p in range(8):
        row = p if p < 4 else 4 * (p // 2 - 1) + 2 * c + p % 2
        base = row * 128 + p * 16
        ids = [sm_i[row, k] for k in range(16)]
        values = [
            lax.shift_left(lax.shift_right_logical(n, 4), 11) + (base + k)
            for k, n in enumerate(ids)
        ]
        hits = [jnp.where((n & 15) == wanted, 1, 0) for n in ids]
        for value, hit in zip(values, hits):
            codes[found] = value
            found = found + hit
    for j in range(STEP - 1):
        codes[found + j] = -1

    def several(i, carry):
        code = [codes[i * STEP + j] for j in range(STEP)]
        used = [jnp.where(n >= 0, 1.0, 0.0) for n in code]
        code = [jnp.maximum(n, 0) for n in code]
        ps = [lax.shift_right_logical(n, 4) & 7 for n in code]
        zs = [lax.shift_right_logical(n, 11) for n in code]
        weights = [sm_f[lax.shift_right_logical(n, 7) & 15, n & 15] * u for n, u in zip(code, used)]
        inter = [
            jnp.dot(
                left[pl.ds(pl.multiple_of(p * v, v), v), :],
                q[zq, :nv, :],
                preferred_element_type=jnp.float32,
            ).astype(jnp.bfloat16)
            for p, zq in zip(ps, zs)
        ]
        mid = [
            jnp.dot(a, q[zq, nv:, :], preferred_element_type=jnp.float32).astype(jnp.bfloat16)
            for a, zq in zip(inter, zs)
        ]
        proj = [
            lax.dot_general(m, a, (((1,), (1,)), ((), ())), preferred_element_type=jnp.float32)
            .astype(jnp.bfloat16)
            .astype(jnp.float32)
            for m, a in zip(mid, inter)
        ]
        for weight, p, value in zip(weights, ps, proj):
            acc[p] += weight * value
        return carry

    lax.fori_loop(0, (found + STEP - 1) // STEP, several, 0)
    near[...] = acc[:4].astype(jnp.bfloat16)
    own[...] = acc[4:6]
    far[...] = acc[6:8].astype(jnp.bfloat16)


def settle_kernel(where, local, near, far, own, kept, gone):
    c = where[3]
    for s in range(2):
        gone[s] = local[2 * (1 - c) + s] - near[2 * (1 - c) + s].astype(jnp.float32)
        kept[s] = local[2 * c + s] - near[2 * c + s].astype(jnp.float32) - (
            own[s] + far[s].astype(jnp.float32)
        )


def shards(
    amplitudes,
    coefficients,
    energies,
    pair_shift,
    pno_count,
    coupled_pairs,
    coupling_weight,
    slab_one,
    slab_two,
):
    pairs, v, _ = amplitudes.shape
    nv = coefficients.shape[1]
    nz = lax.axis_size("z")
    where = jnp.stack([lax.axis_index(a) for a in ("z", "x", "y", "c")]).astype(jnp.int32)
    c = where[3]
    smem = pl.BlockSpec(memory_space=pltpu.SMEM)
    vmem = pl.BlockSpec(memory_space=pltpu.VMEM)
    anywhere = pl.BlockSpec(memory_space=pl.ANY)
    bf16, f32, i32 = jnp.bfloat16, jnp.float32, jnp.int32

    small = pltpu.CompilerParams(vmem_limit_bytes=4 * 1024 * 1024)
    half, amp_half = nv // NC, v // NC
    z_full, x_all, x_own = pl.pallas_call(
        prepare_kernel,
        out_shape=(
            jax.ShapeDtypeStruct((nv + v, v), bf16),
            jax.ShapeDtypeStruct((4 * nv + META, v), bf16),
            jax.ShapeDtypeStruct((2 * nv + META, v), bf16),
        ),
        in_specs=[anywhere] * 4,
        out_specs=(vmem,) * 3,
        scratch_shapes=[
            pltpu.VMEM(coupled_pairs.shape, i32),
            pltpu.VMEM(coupling_weight.shape, f32),
            pltpu.SemaphoreType.DMA((12,)),
        ],
        compiler_params=pltpu.CompilerParams(vmem_limit_bytes=62 * 1024 * 1024),
        name="prepare",
    )(coupled_pairs, coupling_weight, coefficients, amplitudes)

    swap = ring(NC, 1)
    z_one = lax.ppermute(z_full, ("z", "c"), opposite(nz, 1))
    z_two = lax.ppermute(z_full, ("z", "c"), opposite(nz, 2))
    x_near = lax.ppermute(x_all, ("x", "c"), opposite(NX, 1))
    x_far = lax.ppermute(x_own, "x", ring(NX, 2))

    exchange = jnp.einsum("pqa,pqb->pab", slab_one, slab_two, preferred_element_type=f32)
    amp_float = amplitudes.astype(f32)
    right = jnp.einsum("pab,pbc->pac", exchange, amp_float, precision=lax.Precision.HIGHEST)
    quadratic = jnp.einsum("pba,pbc->pac", amp_float, right, precision=lax.Precision.HIGHEST)
    local = exchange + quadratic

    z_three = lax.ppermute(z_two, ("z", "c"), opposite(nz, 1))
    z_four = lax.dynamic_slice_in_dim(z_two, c * (half + amp_half), half + amp_half, 0)
    z_four = lax.ppermute(z_four, ("z", "c"), opposite(nz, 2))
    z_mine = [z_one, z_two, z_three, z_four]
    z_other = [lax.ppermute(b, "c", swap) for b in z_mine]

    near, far, own = pl.pallas_call(
        couple_kernel,
        out_shape=(
            jax.ShapeDtypeStruct((4, v, v), bf16),
            jax.ShapeDtypeStruct((2, v, v), bf16),
            jax.ShapeDtypeStruct((2, v, v), f32),
        ),
        in_specs=[smem] + [vmem] * 12,
        out_specs=(vmem, vmem, vmem),
        scratch_shapes=[
            pltpu.VMEM((8 * v, nv), bf16),
            pltpu.VMEM((nz, nv + v, v), bf16),
            pltpu.VMEM((8, v, v), f32),
            pltpu.VMEM((16, v), f32),
            pltpu.VMEM((16, v), i32),
            pltpu.SMEM((16, v), f32),
            pltpu.SMEM((16, v), i32),
            pltpu.SMEM((136,), i32),
            pltpu.SemaphoreType.DMA((2,)),
        ],
        compiler_params=pltpu.CompilerParams(vmem_limit_bytes=8 * 1024 * 1024),
        cost_estimate=pl.CostEstimate(flops=0, bytes_accessed=12_000_000, transcendentals=0),
        name="couple",
    )(where, x_near, x_own, x_far, z_full, *z_mine, *z_other)

    near_back = lax.ppermute(near, ("x", "c"), opposite(NX, NX - 1))
    far_back = lax.ppermute(far, "x", ring(NX, 2))
    kept, gone = pl.pallas_call(
        settle_kernel,
        out_shape=(jax.ShapeDtypeStruct((2, v, v), f32),) * 2,
        in_specs=[smem] + [vmem] * 4,
        out_specs=(vmem, vmem),
        compiler_params=pltpu.CompilerParams(vmem_limit_bytes=4 * 1024 * 1024),
        name="settle",
    )(where, local, near_back, far_back, own)
    share = kept + lax.ppermute(gone, "c", swap)
    share = share + lax.ppermute(share, ("y", "c"), partners(0))
    share = share + lax.ppermute(share, ("y", "c"), partners(1))
    other = lax.ppermute(share, "c", swap)
    total = jnp.where(
        c == 0, jnp.concatenate([share, other], axis=0), jnp.concatenate([other, share], axis=0)
    )
    diagonal = (energies[:, :, None] + energies[:, None, :] - pair_shift[:, None, None]) * amp_float
    inside = jnp.arange(v, dtype=i32)[None, :] < pno_count[:, None]
    return jnp.where(inside[:, :, None] & inside[:, None, :], total + diagonal, f32(0.0))


def solution(mesh):
    owners = mesh.devices.shape[0]
    fine = Mesh(mesh.devices.reshape(owners // NX, NX, NY, NC), ("z", "x", "y", "c"))
    pair, aux = ("z", "x"), ("y", "c")
    placed = (
        P(pair, None, None),
        P(pair, None, None),
        P(pair, None),
        P(pair),
        P(pair),
        P(pair, None),
        P(pair, None),
        P(pair, aux, None),
        P(pair, aux, None),
    )
    return jax.shard_map(
        shards, mesh=fine, in_specs=placed, out_specs=P(pair, None, None), check_vma=False
    )
```
